768 devices in a mesh: row: 12 (over z), col: 64 (over x, y, core).
Axes of the slice: x: 4, y: 8, z: 12, core: 2. Of those that a mesh axis runs over, the one named last changes fastest.
Arguments:
- x_band: float32 [4608, 64, 448], P(('row', 'col')), may hold values from -0.25 to 0.25
- x_mask: int32 [4608, 7], P(('row', 'col')), may hold values 0 or 1
- g_mask: int32 [4608, 7], P(('row', 'col')), may hold values 0 or 1
Outputs:
- z_band: float32 [4608, 64, 448], P(('row', 'col'))
The draws below stay inside these ranges and needn't reach their ends.
All inputs are finite; a program needn't handle non-finite values. No bound on the sum of `x_mask` or of `g_mask` on one device may be relied on, other than what follows from the above.
Results may differ from the reference program's by a relative error of at most 0.0001.
Values sent between devices are 32-bit elements; how exact they have to be, the bound alone decides.
A program may use at most 64 MiB of HBM per device.

```python
import jax
import jax.numpy as jnp
from jax import lax

BS = 64
HALF = 3
W = 7
NB = 4608


def plant(array, stream_key, least, largest):
    place = [jax.random.randint(jax.random.fold_in(stream_key, axis), (), 0, length) for axis, length in enumerate(array.shape)]
    widest = array.shape.index(max(array.shape))
    beside = place[:widest] + [(place[widest] + 1) % array.shape[widest]] + place[widest + 1:]
    return array.at[tuple(place)].set(least).at[tuple(beside)].set(largest)


def block_levels(rng, dims, split, smallest, top_value):
    loudness, own = 1.0, jax.random.fold_in(rng, 6)
    for dim, blocks in split:
        steps = jnp.exp(jax.random.uniform(jax.random.fold_in(own, dim), (blocks,), jnp.float32, smallest / len(split), top_value / len(split)))
        loudness = loudness * jnp.repeat(steps, dims[dim] // blocks).reshape([-1 if axis == dim else 1 for axis in range(len(dims))])
    return loudness


def noise(stream_key, extent, deviation, reach, split=(), kind=jnp.bfloat16):
    entries = jax.random.normal(stream_key, extent, jnp.float32) * deviation
    if len(split) > 0:
        entries = block_levels(stream_key, extent, split, -0.22, 0.18) * entries
    return jnp.clip(entries, min=-reach, max=reach).astype(kind)


def setup_inputs(seed: int = 0) -> dict:
    key_of = jax.random.split(jax.random.key(seed), 4)
    return {
        "x_band": noise(key_of[0], (NB, BS, W * BS), (W * BS) ** -0.5, 0.25, ((0, 768),), jnp.float32),
        "x_mask": plant((jax.random.randint(key_of[1], (NB, W), 0, 4) < 3).astype(jnp.int32), jax.random.fold_in(key_of[1], 1), 0, 1),
        "g_mask": plant((jax.random.randint(key_of[2], (NB, W), 0, 4) < 3).astype(jnp.int32), jax.random.fold_in(key_of[2], 1), 0, 1),
    }


def band_product(left_band, right_band):
    padded = jnp.pad(right_band, ((0, 0), (0, 0), (HALF, HALF), (0, 0)))

    def advance(running, offset):
        near_rows = jnp.roll(padded, HALF - offset, axis=0)
        window = lax.dynamic_slice_in_dim(near_rows, 2 * HALF - offset, W, 2)
        left_block = lax.dynamic_index_in_dim(left_band, offset, 2, keepdims=False)
        term = jnp.einsum('iac,icub->iaub', left_block, window, precision=lax.Precision.HIGHEST)
        return running + term, None

    zero_sum = jnp.zeros(left_band.shape, jnp.float32)
    running, _ = lax.scan(advance, zero_sum, jnp.arange(W, dtype=jnp.int32))
    return running


def reference(x_band, x_mask, g_mask):
    stored = x_band.reshape(NB, BS, W, BS)
    pattern = x_mask.astype(jnp.float32)[:, None, :, None]
    matrix_x = stored * pattern
    square = band_product(matrix_x, matrix_x) * g_mask.astype(jnp.float32)[:, None, :, None]
    result = (1.5 * matrix_x - 0.5 * band_product(matrix_x, square)) * pattern
    return result.reshape(NB, BS, W * BS)
```

```python
import functools

import jax
import jax.numpy as jnp
from jax import lax
from jax.experimental import pallas as pl
from jax.experimental.pallas import tpu as pltpu
from jax.sharding import PartitionSpec as P

BS = 64
W = 7
ROWS = 6
MESH = pl.DeviceIdType.MESH
F32 = jnp.float32
BF16 = jnp.bfloat16


def split(value):
    high = value.astype(BF16)
    return high, (value - high.astype(F32)).astype(BF16)


def product(left, right):
    lhs = jnp.concatenate([left[0], left[0], left[1]], axis=1)
    rhs = jnp.concatenate([right[0], right[1], right[0]], axis=0)
    return jnp.dot(lhs, rhs, preferred_element_type=F32)


def kernel(
    x_hbm, xm_hbm, gm_hbm, z_hbm,
    x_v, xm_s, gm_s, xp, dh, dl, gh, gl, gacc, x_recv, p_send, p_recv, m_send, m_recv, z_v,
    in_sem, out_sem, send_sem, recv_sem,
):
    rows, cols = lax.axis_size("row"), lax.axis_size("col")
    flat = lax.axis_index("row") * cols + lax.axis_index("col")
    there = []
    for step in (rows * cols - 1, 1):
        other = lax.rem(flat + step, rows * cols)
        there.append((lax.div(other, cols), lax.rem(other, cols)))

    barrier = pltpu.get_barrier_semaphore()
    for device in there:
        pl.semaphore_signal(barrier, inc=1, device_id=device, device_id_type=MESH)

    loads = [pltpu.make_async_copy(xm_hbm, xm_s, in_sem.at[ROWS]), pltpu.make_async_copy(gm_hbm, gm_s, in_sem.at[ROWS + 1])]
    loads += [pltpu.make_async_copy(x_hbm.at[i], x_v.at[i], in_sem.at[i]) for i in range(ROWS)]
    for load in loads:
        load.start()
    for buffer in (dh, dl, gh, gl, m_send):
        buffer[...] = jnp.zeros_like(buffer)

    lane = lax.broadcasted_iota(jnp.int32, (1, 128), 1)
    low = lane < BS

    def window_mask(mask, i):
        def factor(t):
            return mask[i, t].astype(F32) if 0 <= t < W else jnp.float32(0)

        first = -(i % 2)
        return jnp.concatenate(
            [jnp.where(low, factor(first + 2 * u), factor(first + 2 * u + 1)) for u in range(4)], axis=1
        )

    loads[0].wait()
    loads[1].wait()
    blank = jnp.zeros((BS, BS), F32)
    for i in range(ROWS):
        loads[2 + i].wait()
        value = x_v[i]
        value = jnp.concatenate([value, blank] if i % 2 == 0 else [blank, value], axis=1) * window_mask(xm_s, i)
        xp[i] = value
        high, rest = split(value)
        span = slice(192 + 64 * i, 256 + 64 * i), slice(128 * (i // 2), 128 * (i // 2) + 512)
        dh[span] = high
        dl[span] = rest
    for i in range(3):
        ours = window_mask(gm_s, i)
        m_send[0, i : i + 1, 128 * (i // 2) : 384] = ours[:, : 384 - 128 * (i // 2)]
        ours = window_mask(gm_s, 3 + i)
        start = 384 - 128 * ((3 + i) // 2)
        m_send[1, i : i + 1, 0 : 512 - start] = ours[:, start:]

    pl.semaphore_wait(barrier, 2)

    pieces = [
        [
            (xp.at[0:2, :, 0:384], x_recv.at[1, 0:2]),
            (xp.at[2, :, 0:256], x_recv.at[1, 2, :, 128:384]),
            (m_send.at[0], m_recv.at[1]),
            (p_send.at[0], p_recv.at[1]),
        ],
        [
            (xp.at[4:6, :, 128:512], x_recv.at[0, 1:3]),
            (xp.at[3, :, 256:512], x_recv.at[0, 0, :, 0:256]),
            (m_send.at[1], m_recv.at[0]),
            (p_send.at[1], p_recv.at[0]),
        ],
    ]

    def remote(side, number, from_side):
        src, dst = pieces[side][number]
        return pltpu.make_async_remote_copy(
            src_ref=src, dst_ref=dst, send_sem=send_sem.at[side, number], recv_sem=recv_sem.at[from_side, number],
            device_id=there[side], device_id_type=MESH,
        )

    sends = [[remote(side, number, 1 - side) for number in range(4)] for side in (0, 1)]

    def arrived(side, number):
        remote(1 - side, number, side).wait_recv()

    for number in (0, 1, 2):
        for side in (0, 1):
            sends[side][number].start()

    def d(row, height, column, width):
        span = slice(row, row + height), slice(column, column + width)
        return dh[span], dl[span]

    to_left = product(d(192, 192, 384, 256), d(384, 256, 128, 256))
    to_right = product(d(384, 192, 128, 256), d(128, 256, 384, 256))
    for side, whole, half in ((0, to_left[:, 128:], to_left[:, :128]), (1, to_right[:, :128], to_right[:, 128:])):
        p_send[side, 0:192] = whole
        p_send[side, 192:288] = half[0:96] + pltpu.roll(half[96:192], 64, 1)
        sends[side][3].start()

    for p in range(3):
        gacc[p] = product(d(192 + 128 * p, 128, 256, 256), d(256, 256, 128 * p, 512))

    def put_g(row, column, value):
        high, rest = split(value)
        span = slice(row, row + value.shape[0]), slice(column, column + value.shape[1])
        gh[span] = high
        gl[span] = rest

    def put_pair(p, value):
        for i in (2 * p, 2 * p + 1):
            put_g(192 + 64 * i, 128 * p, value[64 * (i % 2) : 64 * (i % 2) + 64] * window_mask(gm_s, i))

    for side in (0, 1):
        arrived(side, 0)
        arrived(side, 1)
        for r in range(3):
            row = 64 * r + 576 * side
            short = (r == 0) if side == 0 else (r == 2)
            if side == 0:
                value, column = (x_recv[0, r, :, 0:256] if short else x_recv[0, r]), 0
            else:
                value, column = (x_recv[1, r, :, 128:384], 512) if short else (x_recv[1, r], 384)
            high, rest = split(value)
            span = slice(row, row + 64), slice(column, column + value.shape[1])
            dh[span] = high
            dl[span] = rest
        if side == 0:
            outer = product(d(0, 448, 0, 256), d(0, 256, 0, 512))
            halo = outer[0:192, 0:384] + product(d(0, 192, 256, 256), d(256, 256, 0, 384))
            put_pair(0, gacc[0] + outer[192:320])
            gacc[1, :, 0:384] += outer[320:448, 128:512]
        else:
            outer = product(d(320, 448, 512, 256), d(512, 256, 256, 512))
            halo = outer[256:448, 128:512] + product(d(576, 192, 256, 256), d(256, 256, 384, 384))
            put_pair(2, gacc[2] + outer[128:256])
            gacc[1, :, 128:512] += outer[0:128, 0:384]
            put_pair(1, gacc[1])
        arrived(side, 2)
        arrived(side, 3)
        whole = p_recv[side, 0:192]
        half = p_recv[side, 192:288]
        half = jnp.concatenate([half, pltpu.roll(half, 64, 1)], axis=0)
        if side == 0:
            extra = [whole, jnp.where(low, half, 0.0), jnp.zeros((192, 128), F32)]
        else:
            extra = [jnp.zeros((192, 128), F32), jnp.where(low, 0.0, half), whole]
        halo = halo + jnp.concatenate(extra, axis=1)
        for r in range(3):
            put_g(64 * r + 576 * side, 384 * side, halo[64 * r : 64 * r + 64] * m_recv[side, r : r + 1])

    def g(row, height, column, width):
        span = slice(row, row + height), slice(column, column + width)
        return gh[span], gl[span]

    stores = []
    for p in range(3):
        cubic = product(d(192 + 128 * p, 128, 128 * p, 512), g(128 * p, 512, 128 * p, 512))
        for i in (2 * p, 2 * p + 1):
            start = 64 * (i % 2)
            z = 1.5 * xp[i] - (0.5 * window_mask(xm_s, i)) * cubic[start : start + 64]
            z_v[i] = z[:, start : start + W * BS]
            stores.append(pltpu.make_async_copy(z_v.at[i], z_hbm.at[i], out_sem.at[i]))
            stores[-1].start()

    for side in (0, 1):
        for copy in sends[side]:
            copy.wait_send()
    for store in stores:
        store.wait()


def body(x_band, x_mask, g_mask):
    return pl.pallas_call(
        kernel,
        out_shape=jax.ShapeDtypeStruct(x_band.shape, F32),
        in_specs=[pl.BlockSpec(memory_space=pl.ANY)] * 3,
        out_specs=pl.BlockSpec(memory_space=pl.ANY),
        scratch_shapes=[
            pltpu.VMEM((ROWS, BS, W * BS), F32),
            pltpu.SMEM((ROWS, W), jnp.int32),
            pltpu.SMEM((ROWS, W), jnp.int32),
            pltpu.VMEM((ROWS, BS, 512), F32),
            pltpu.VMEM((768, 768), BF16),
            pltpu.VMEM((768, 768), BF16),
            pltpu.VMEM((768, 768), BF16),
            pltpu.VMEM((768, 768), BF16),
            pltpu.VMEM((3, 128, 512), F32),
            pltpu.VMEM((2, 3, BS, 384), F32),
            pltpu.VMEM((2, 288, 128), F32),
            pltpu.VMEM((2, 288, 128), F32),
            pltpu.VMEM((2, 8, 384), F32),
            pltpu.VMEM((2, 8, 384), F32),
            pltpu.VMEM((ROWS, BS, W * BS), F32),
            pltpu.SemaphoreType.DMA((ROWS + 2,)),
            pltpu.SemaphoreType.DMA((ROWS,)),
            pltpu.SemaphoreType.DMA((2, 4)),
            pltpu.SemaphoreType.DMA((2, 4)),
        ],
        compiler_params=pltpu.CompilerParams(
            collective_id=0, has_side_effects=True, vmem_limit_bytes=48 * 1024 * 1024
        ),
        cost_estimate=pl.CostEstimate(flops=1_000_000_000, bytes_accessed=1_500_000, transcendentals=0),
    )(x_band, x_mask, g_mask)


def solution(mesh):
    placed = (P(("row", "col"), None, None), P(("row", "col"), None), P(("row", "col"), None))
    return jax.shard_map(
        body, mesh=mesh, in_specs=placed, out_specs=P(("row", "col"), None, None), check_vma=False
    )
```

```python
import functools

import jax
import jax.numpy as jnp
from jax import lax
from jax.experimental import pallas as pl
from jax.experimental.pallas import tpu as pltpu
from jax.sharding import PartitionSpec as P

BS = 64
W = 7
ROWS = 6
MESH = pl.DeviceIdType.MESH
F32 = jnp.float32
BF16 = jnp.bfloat16


def split(value):
    high = value.astype(BF16)
    return high, (value - high.astype(F32)).astype(BF16)


def product(left, right):
    lhs = jnp.concatenate([left[0], left[0], left[1]], axis=1)
    rhs = jnp.concatenate([right[0], right[1], right[0]], axis=0)
    return jnp.dot(lhs, rhs, preferred_element_type=F32)


def kernel(
    x_hbm, xm_hbm, gm_hbm, z_out,
    x_v, xm_s, gm_s, xp, dh, dl, gh, gl, gacc, x_recv, p_send, p_recv, m_send, m_recv,
    zacc, in_sem, send_sem, recv_sem, left_here,
):
    rows, cols = lax.axis_size("row"), lax.axis_size("col")
    flat = lax.axis_index("row") * cols + lax.axis_index("col")
    there = []
    for step in (rows * cols - 1, 1):
        other = lax.rem(flat + step, rows * cols)
        there.append((lax.div(other, cols), lax.rem(other, cols)))

    barrier = pltpu.get_barrier_semaphore()
    pl.semaphore_signal(barrier, inc=1, device_id=there[0], device_id_type=MESH)

    order = (3, 4, 5, 0, 1, 2)
    loads = [pltpu.make_async_copy(x_hbm.at[i], x_v.at[i], in_sem.at[i]) for i in range(ROWS)]
    mask_loads = [pltpu.make_async_copy(xm_hbm, xm_s, in_sem.at[ROWS]), pltpu.make_async_copy(gm_hbm, gm_s, in_sem.at[ROWS + 1])]
    for load in mask_loads:
        load.start()
    for i in order:
        loads[i].start()
    for buffer in (dh, dl, m_send):
        buffer[...] = jnp.zeros_like(buffer)

    lane = lax.broadcasted_iota(jnp.int32, (1, 128), 1)
    low = lane < BS

    def window_mask(mask, i):
        def factor(t):
            return mask[i, t].astype(F32) if 0 <= t < W else jnp.float32(0)

        first = -(i % 2)
        return jnp.concatenate(
            [jnp.where(low, factor(first + 2 * u), factor(first + 2 * u + 1)) for u in range(4)], axis=1
        )

    pieces = [
        [
            (xp.at[0:2, :, 0:384], x_recv.at[1, 0:2]),
            (xp.at[2, :, 0:256], x_recv.at[1, 2, :, 128:384]),
            (m_send.at[0], m_recv.at[1]),
            (p_send.at[0], p_recv.at[1]),
        ],
        [
            (xp.at[4:6, :, 128:512], x_recv.at[0, 1:3]),
            (xp.at[3, :, 256:512], x_recv.at[0, 0, :, 0:256]),
            (m_send.at[1], m_recv.at[0]),
            (p_send.at[1], p_recv.at[0]),
        ],
    ]

    def remote(side, number, from_side):
        src, dst = pieces[side][number]
        return pltpu.make_async_remote_copy(
            src_ref=src, dst_ref=dst, send_sem=send_sem.at[side, number], recv_sem=recv_sem.at[from_side, number],
            device_id=there[side], device_id_type=MESH,
        )

    sends = [[remote(side, number, 1 - side) for number in range(4)] for side in (0, 1)]

    def arrived(side, number):
        remote(1 - side, number, side).wait_recv()

    blank = jnp.zeros((BS, BS), F32)

    def prepare(i):
        loads[i].wait()
        value = x_v[i]
        value = jnp.concatenate([value, blank] if i % 2 == 0 else [blank, value], axis=1) * window_mask(xm_s, i)
        xp[i] = value
        high, rest = split(value)
        span = slice(192 + 64 * i, 256 + 64 * i), slice(128 * (i // 2), 128 * (i // 2) + 512)
        dh[span] = high
        dl[span] = rest

    def d(row, height, column, width):
        span = slice(row, row + height), slice(column, column + width)
        return dh[span], dl[span]

    def g(row, height, column, width):
        span = slice(row, row + height), slice(column, column + width)
        return gh[span], gl[span]

    for load in mask_loads:
        load.wait()
    for i in (3, 4, 5):
        prepare(i)
        start = 384 - 128 * (i // 2)
        m_send[1, i - 3 : i - 2, 0 : 512 - start] = window_mask(gm_s, i)[:, start:]
    pl.semaphore_wait(barrier, 1)
    pl.semaphore_signal(left_here, inc=1, device_id=there[1], device_id_type=MESH)
    for number in (0, 1, 2):
        sends[1][number].start()
    for i in (0, 1, 2):
        prepare(i)
        m_send[0, i : i + 1, 128 * (i // 2) : 384] = window_mask(gm_s, i)[:, : 384 - 128 * (i // 2)]

    to_right = product(d(384, 192, 128, 256), d(128, 256, 384, 256))
    p_send[1, 0:192] = to_right[:, :128]
    p_send[1, 192:288] = to_right[0:96, 128:] + pltpu.roll(to_right[96:192, 128:], 64, 1)
    sends[1][3].start()
    to_left = product(d(192, 192, 384, 256), d(384, 256, 128, 256))
    p_send[0, 0:192] = to_left[:, 128:]
    p_send[0, 192:288] = to_left[0:96, :128] + pltpu.roll(to_left[96:192, :128], 64, 1)

    pl.semaphore_wait(left_here, 1)
    for number in range(4):
        sends[0][number].start()

    for buffer in (gh, gl):
        buffer[...] = jnp.zeros_like(buffer)
    for p in range(3):
        gacc[p] = product(d(192 + 128 * p, 128, 256, 256), d(256, 256, 128 * p, 512))

    def put_g(row, column, value):
        high, rest = split(value)
        span = slice(row, row + value.shape[0]), slice(column, column + value.shape[1])
        gh[span] = high
        gl[span] = rest

    def put_pair(p, value):
        for i in (2 * p, 2 * p + 1):
            put_g(192 + 64 * i, 128 * p, value[64 * (i % 2) : 64 * (i % 2) + 64] * window_mask(gm_s, i))

    def take_x(side):
        arrived(side, 0)
        arrived(side, 1)
        for r in range(3):
            short = (r == 0) if side == 0 else (r == 2)
            if side == 0:
                value, column = (x_recv[0, r, :, 0:256] if short else x_recv[0, r]), 0
            else:
                value, column = (x_recv[1, r, :, 128:384], 512) if short else (x_recv[1, r], 384)
            high, rest = split(value)
            span = slice(64 * r + 576 * side, 64 * r + 576 * side + 64), slice(column, column + value.shape[1])
            dh[span] = high
            dl[span] = rest

    def take_p(side, halo):
        arrived(side, 2)
        arrived(side, 3)
        whole = p_recv[side, 0:192]
        half = p_recv[side, 192:288]
        half = jnp.concatenate([half, pltpu.roll(half, 64, 1)], axis=0)
        if side == 0:
            sums = [halo[:, 0:128] + whole, halo[:, 128:256] + jnp.where(low, half, 0.0), halo[:, 256:384]]
        else:
            sums = [halo[:, 0:128], halo[:, 128:256] + jnp.where(low, 0.0, half), halo[:, 256:384] + whole]
        halo = jnp.concatenate(sums, axis=1)
        for r in range(3):
            put_g(64 * r + 576 * side, 384 * side, halo[64 * r : 64 * r + 64] * m_recv[side, r : r + 1])

    def finish(p, cubic):
        for i in (2 * p, 2 * p + 1):
            start = 64 * (i % 2)
            z = 1.5 * xp[i] - (0.5 * window_mask(xm_s, i)) * cubic[start : start + 64]
            z_out[i] = z[:, start : start + W * BS]

    take_x(1)
    outer = product(d(320, 448, 512, 256), d(512, 256, 256, 512))
    halo = outer[256:448, 128:512] + product(d(576, 192, 256, 256), d(256, 256, 384, 384))
    gacc[1, :, 128:512] += outer[0:128, 0:384]
    put_pair(2, gacc[2] + outer[128:256])
    take_p(1, halo)
    cubic = product(d(320, 256, 512, 256), g(512, 256, 256, 512))
    zacc[1, :, 0:128] = jnp.zeros((128, 128), F32)
    zacc[1, :, 128:512] = cubic[0:128, 0:384]
    zacc[2] = cubic[128:256]

    take_x(0)
    outer = product(d(0, 448, 0, 256), d(0, 256, 0, 512))
    put_pair(0, gacc[0] + outer[192:320])
    gacc[1, :, 0:384] += outer[320:448, 128:512]
    put_pair(1, gacc[1])
    halo = outer[0:192, 0:384] + product(d(0, 192, 256, 256), d(256, 256, 0, 384))
    zacc[0] = product(d(192, 128, 256, 256), g(256, 256, 0, 512))
    zacc[1] += product(d(320, 128, 256, 256), g(256, 256, 128, 512))
    finish(2, zacc[2] + product(d(448, 128, 256, 256), g(256, 256, 256, 512)))
    take_p(0, halo)
    cubic = product(d(192, 256, 0, 256), g(0, 256, 0, 512))
    finish(0, zacc[0] + cubic[0:128])
    zacc[1, :, 0:384] += cubic[128:256, 128:512]
    finish(1, zacc[1])

    for side in (0, 1):
        for copy in sends[side]:
            copy.wait_send()


def body(x_band, x_mask, g_mask):
    return pl.pallas_call(
        kernel,
        out_shape=jax.ShapeDtypeStruct(x_band.shape, F32),
        in_specs=[pl.BlockSpec(memory_space=pltpu.HBM)] * 3,
        out_specs=pl.BlockSpec(memory_space=pltpu.VMEM),
        scratch_shapes=[
            pltpu.VMEM((ROWS, BS, W * BS), F32),
            pltpu.SMEM((ROWS, W), jnp.int32),
            pltpu.SMEM((ROWS, W), jnp.int32),
            pltpu.VMEM((ROWS, BS, 512), F32),
            pltpu.VMEM((768, 768), BF16),
            pltpu.VMEM((768, 768), BF16),
            pltpu.VMEM((768, 768), BF16),
            pltpu.VMEM((768, 768), BF16),
            pltpu.VMEM((3, 128, 512), F32),
            pltpu.VMEM((2, 3, BS, 384), F32),
            pltpu.VMEM((2, 288, 128), F32),
            pltpu.VMEM((2, 288, 128), F32),
            pltpu.VMEM((2, 8, 384), F32),
            pltpu.VMEM((2, 8, 384), F32),
            pltpu.VMEM((3, 128, 512), F32),
            pltpu.SemaphoreType.DMA((ROWS + 2,)),
            pltpu.SemaphoreType.DMA((2, 4)),
            pltpu.SemaphoreType.DMA((2, 4)),
            pltpu.SemaphoreType.REGULAR,
        ],
        compiler_params=pltpu.CompilerParams(
            collective_id=0, has_side_effects=True, vmem_limit_bytes=48 * 1024 * 1024
        ),
        cost_estimate=pl.CostEstimate(flops=1_000_000_000, bytes_accessed=1_500_000, transcendentals=0),
    )(*(pltpu.with_memory_space_constraint(a, pltpu.HBM) for a in (x_band, x_mask, g_mask)))


def solution(mesh):
    placed = (P(("row", "col"), None, None), P(("row", "col"), None), P(("row", "col"), None))
    return jax.shard_map(
        body, mesh=mesh, in_specs=placed, out_specs=P(("row", "col"), None, None), check_vma=False
    )
```

```python
import functools

import jax
import jax.numpy as jnp
from jax import lax
from jax.experimental import pallas as pl
from jax.experimental.pallas import tpu as pltpu
from jax.sharding import PartitionSpec as P

BS = 64
W = 7
ROWS = 6
MESH = pl.DeviceIdType.MESH
F32 = jnp.float32
BF16 = jnp.bfloat16


def split(value):
    high = value.astype(BF16)
    return high, (value - high.astype(F32)).astype(BF16)


def product(left, right):
    lhs = jnp.concatenate([left[0], left[0], left[1]], axis=1)
    rhs = jnp.concatenate([right[0], right[1], right[0]], axis=0)
    return jnp.dot(lhs, rhs, preferred_element_type=F32)


def kernel(
    x_hbm, xm_hbm, gm_hbm, z_out,
    x_v, xm_s, gm_s, xp, dh, dl, gh, gl, gacc, x_recv, p_send, p_recv, m_send, m_recv,
    zacc, in_sem, send_sem, recv_sem, left_here,
):
    rows, cols = lax.axis_size("row"), lax.axis_size("col")
    flat = lax.axis_index("row") * cols + lax.axis_index("col")
    there = []
    for step in (rows * cols - 1, 1):
        other = lax.rem(flat + step, rows * cols)
        there.append((lax.div(other, cols), lax.rem(other, cols)))

    first_two = flat < 2
    barrier = pltpu.get_barrier_semaphore()
    pl.semaphore_signal(barrier, inc=1, device_id=there[0], device_id_type=MESH)
    replies = jnp.logical_or(flat == 0, flat == rows * cols - 1)

    @pl.when(jnp.logical_not(replies))
    def _():
        pl.semaphore_signal(barrier, inc=1, device_id=there[1], device_id_type=MESH)

    order = (3, 4, 5, 0, 1, 2)
    loads = [pltpu.make_async_copy(x_hbm.at[i], x_v.at[i], in_sem.at[i]) for i in range(ROWS)]
    mask_loads = [pltpu.make_async_copy(xm_hbm, xm_s, in_sem.at[ROWS]), pltpu.make_async_copy(gm_hbm, gm_s, in_sem.at[ROWS + 1])]
    for load in mask_loads:
        load.start()
    for i in order:
        loads[i].start()
    for buffer in (dh, dl, m_send):
        buffer[...] = jnp.zeros_like(buffer)

    @pl.when(replies)
    def _():
        pl.semaphore_wait(barrier, jnp.where(flat == 0, 1, 2))
        pl.semaphore_signal(left_here, inc=1, device_id=there[1], device_id_type=MESH)

    lane = lax.broadcasted_iota(jnp.int32, (1, 128), 1)
    low = lane < BS

    def window_mask(mask, i):
        def factor(t):
            return mask[i, t].astype(F32) if 0 <= t < W else jnp.float32(0)

        first = -(i % 2)
        return jnp.concatenate(
            [jnp.where(low, factor(first + 2 * u), factor(first + 2 * u + 1)) for u in range(4)], axis=1
        )

    pieces = [
        [
            (xp.at[0:2, :, 0:384], x_recv.at[1, 0:2]),
            (xp.at[2, :, 0:256], x_recv.at[1, 2, :, 128:384]),
            (m_send.at[0], m_recv.at[1]),
            (p_send.at[0], p_recv.at[1]),
        ],
        [
            (xp.at[4:6, :, 128:512], x_recv.at[0, 1:3]),
            (xp.at[3, :, 256:512], x_recv.at[0, 0, :, 0:256]),
            (m_send.at[1], m_recv.at[0]),
            (p_send.at[1], p_recv.at[0]),
        ],
    ]

    def remote(side, number, from_side):
        src, dst = pieces[side][number]
        return pltpu.make_async_remote_copy(
            src_ref=src, dst_ref=dst, send_sem=send_sem.at[side, number], recv_sem=recv_sem.at[from_side, number],
            device_id=there[side], device_id_type=MESH,
        )

    sends = [[remote(side, number, 1 - side) for number in range(4)] for side in (0, 1)]

    def arrived(side, number):
        remote(1 - side, number, side).wait_recv()

    blank = jnp.zeros((BS, BS), F32)

    def prepare(i):
        loads[i].wait()
        value = x_v[i]
        value = jnp.concatenate([value, blank] if i % 2 == 0 else [blank, value], axis=1) * window_mask(xm_s, i)
        xp[i] = value
        high, rest = split(value)
        span = slice(192 + 64 * i, 256 + 64 * i), slice(128 * (i // 2), 128 * (i // 2) + 512)
        dh[span] = high
        dl[span] = rest

    def d(row, height, column, width):
        span = slice(row, row + height), slice(column, column + width)
        return dh[span], dl[span]

    def g(row, height, column, width):
        span = slice(row, row + height), slice(column, column + width)
        return gh[span], gl[span]

    for load in mask_loads:
        load.wait()
    for i in (3, 4, 5):
        prepare(i)
        start = 384 - 128 * (i // 2)
        m_send[1, i - 3 : i - 2, 0 : 512 - start] = window_mask(gm_s, i)[:, start:]

    @pl.when(jnp.logical_not(replies))
    def _():
        pl.semaphore_wait(barrier, jnp.where(flat == 1, 1, 2))

    for number in (0, 1, 2):
        sends[1][number].start()
    for i in (0, 1, 2):
        prepare(i)
        m_send[0, i : i + 1, 128 * (i // 2) : 384] = window_mask(gm_s, i)[:, : 384 - 128 * (i // 2)]

    @pl.when(jnp.logical_not(first_two))
    def _():
        for number in (0, 1, 2):
            sends[0][number].start()

    to_right = product(d(384, 192, 128, 256), d(128, 256, 384, 256))
    p_send[1, 0:192] = to_right[:, :128]
    p_send[1, 192:288] = to_right[0:96, 128:] + pltpu.roll(to_right[96:192, 128:], 64, 1)
    sends[1][3].start()
    to_left = product(d(192, 192, 384, 256), d(384, 256, 128, 256))
    p_send[0, 0:192] = to_left[:, 128:]
    p_send[0, 192:288] = to_left[0:96, :128] + pltpu.roll(to_left[96:192, :128], 64, 1)

    @pl.when(jnp.logical_not(first_two))
    def _():
        sends[0][3].start()

    for buffer in (gh, gl):
        buffer[...] = jnp.zeros_like(buffer)
    for p in range(3):
        gacc[p] = product(d(192 + 128 * p, 128, 256, 256), d(256, 256, 128 * p, 512))

    def put_g(row, column, value):
        high, rest = split(value)
        span = slice(row, row + value.shape[0]), slice(column, column + value.shape[1])
        gh[span] = high
        gl[span] = rest

    def put_pair(p, value):
        for i in (2 * p, 2 * p + 1):
            put_g(192 + 64 * i, 128 * p, value[64 * (i % 2) : 64 * (i % 2) + 64] * window_mask(gm_s, i))

    def take_x(side):
        arrived(side, 0)
        arrived(side, 1)
        for r in range(3):
            short = (r == 0) if side == 0 else (r == 2)
            if side == 0:
                value, column = (x_recv[0, r, :, 0:256] if short else x_recv[0, r]), 0
            else:
                value, column = (x_recv[1, r, :, 128:384], 512) if short else (x_recv[1, r], 384)
            high, rest = split(value)
            span = slice(64 * r + 576 * side, 64 * r + 576 * side + 64), slice(column, column + value.shape[1])
            dh[span] = high
            dl[span] = rest

    def take_p(side, halo):
        arrived(side, 2)
        arrived(side, 3)
        whole = p_recv[side, 0:192]
        half = p_recv[side, 192:288]
        half = jnp.concatenate([half, pltpu.roll(half, 64, 1)], axis=0)
        if side == 0:
            sums = [halo[:, 0:128] + whole, halo[:, 128:256] + jnp.where(low, half, 0.0), halo[:, 256:384]]
        else:
            sums = [halo[:, 0:128], halo[:, 128:256] + jnp.where(low, 0.0, half), halo[:, 256:384] + whole]
        halo = jnp.concatenate(sums, axis=1)
        for r in range(3):
            put_g(64 * r + 576 * side, 384 * side, halo[64 * r : 64 * r + 64] * m_recv[side, r : r + 1])

    def finish(p, cubic):
        for i in (2 * p, 2 * p + 1):
            start = 64 * (i % 2)
            z = 1.5 * xp[i] - (0.5 * window_mask(xm_s, i)) * cubic[start : start + 64]
            z_out[i] = z[:, start : start + W * BS]

    def over(side):
        take_x(side)
        if side == 0:
            outer = product(d(0, 448, 0, 256), d(0, 256, 0, 512))
            return outer[192:320], outer[320:448, 128:512], outer[0:192, 0:384]
        outer = product(d(320, 448, 512, 256), d(512, 256, 256, 512))
        return outer[128:256], outer[0:128, 0:384], outer[256:448, 128:512]

    def halo_over(side):
        if side == 0:
            return product(d(0, 192, 256, 256), d(256, 256, 0, 384))
        return product(d(576, 192, 256, 256), d(256, 256, 384, 384))

    def cubic_over(side):
        if side == 0:
            cubic = product(d(192, 256, 0, 256), g(0, 256, 0, 512))
            return cubic[0:128], cubic[128:256, 128:512]
        cubic = product(d(320, 256, 512, 256), g(512, 256, 256, 512))
        return cubic[128:256], cubic[0:128, 0:384]

    def cubic_within(p):
        return product(d(192 + 128 * p, 128, 256, 256), g(256, 256, 128 * p, 512))

    def both_sides(first):
        last = 1 - first
        near, far = (slice(0, 384), slice(128, 512)) if first == 0 else (slice(128, 512), slice(0, 384))
        edge, middle, halo = over(first)
        gacc[1, :, near] += middle
        put_pair(2 * first, gacc[2 * first] + edge)
        take_p(first, halo + halo_over(first))
        edge, middle = cubic_over(first)
        zacc[2 * first] = edge
        zacc[1] = jnp.zeros((128, 512), F32)
        zacc[1, :, near] = middle

        @pl.when(first_two)
        def _():
            pl.semaphore_wait(left_here, 1)
            for number in range(4):
                sends[0][number].start()

        edge, middle, halo = over(last)
        put_pair(2 * last, gacc[2 * last] + edge)
        gacc[1, :, far] += middle
        put_pair(1, gacc[1])
        halo += halo_over(last)
        finish(2 * first, zacc[2 * first] + cubic_within(2 * first))
        zacc[2 * last] = cubic_within(2 * last)
        zacc[1] += cubic_within(1)
        take_p(last, halo)
        edge, middle = cubic_over(last)
        finish(2 * last, zacc[2 * last] + edge)
        zacc[1, :, far] += middle
        finish(1, zacc[1])

    right_last = jnp.logical_and(lax.rem(flat, 2) == 1, flat != 1)

    @pl.when(jnp.logical_not(right_last))
    def _():
        both_sides(1)

    @pl.when(right_last)
    def _():
        both_sides(0)

    for side in (0, 1):
        for copy in sends[side]:
            copy.wait_send()


def body(x_band, x_mask, g_mask):
    return pl.pallas_call(
        kernel,
        out_shape=jax.ShapeDtypeStruct(x_band.shape, F32),
        in_specs=[pl.BlockSpec(memory_space=pltpu.HBM)] * 3,
        out_specs=pl.BlockSpec(memory_space=pltpu.VMEM),
        scratch_shapes=[
            pltpu.VMEM((ROWS, BS, W * BS), F32),
            pltpu.SMEM((ROWS, W), jnp.int32),
            pltpu.SMEM((ROWS, W), jnp.int32),
            pltpu.VMEM((ROWS, BS, 512), F32),
            pltpu.VMEM((768, 768), BF16),
            pltpu.VMEM((768, 768), BF16),
            pltpu.VMEM((768, 768), BF16),
            pltpu.VMEM((768, 768), BF16),
            pltpu.VMEM((3, 128, 512), F32),
            pltpu.VMEM((2, 3, BS, 384), F32),
            pltpu.VMEM((2, 288, 128), F32),
            pltpu.VMEM((2, 288, 128), F32),
            pltpu.VMEM((2, 8, 384), F32),
            pltpu.VMEM((2, 8, 384), F32),
            pltpu.VMEM((3, 128, 512), F32),
            pltpu.SemaphoreType.DMA((ROWS + 2,)),
            pltpu.SemaphoreType.DMA((2, 4)),
            pltpu.SemaphoreType.DMA((2, 4)),
            pltpu.SemaphoreType.REGULAR,
        ],
        compiler_params=pltpu.CompilerParams(
            collective_id=0, has_side_effects=True, vmem_limit_bytes=48 * 1024 * 1024
        ),
        cost_estimate=pl.CostEstimate(flops=1_000_000_000, bytes_accessed=1_500_000, transcendentals=0),
    )(*(pltpu.with_memory_space_constraint(a, pltpu.HBM) for a in (x_band, x_mask, g_mask)))


def solution(mesh):
    placed = (P(("row", "col"), None, None), P(("row", "col"), None), P(("row", "col"), None))
    return jax.shard_map(
        body, mesh=mesh, in_specs=placed, out_specs=P(("row", "col"), None, None), check_vma=False
    )
```

```python
import functools

import jax
import jax.numpy as jnp
from jax import lax
from jax.experimental import pallas as pl
from jax.experimental.pallas import tpu as pltpu
from jax.sharding import PartitionSpec as P

BS = 64
W = 7
ROWS = 6
MESH = pl.DeviceIdType.MESH
F32 = jnp.float32
BF16 = jnp.bfloat16


def split(value):
    high = value.astype(BF16)
    return high, (value - high.astype(F32)).astype(BF16)


def product(left, right):
    lhs = jnp.concatenate([left[0], left[0], left[1]], axis=1)
    rhs = jnp.concatenate([right[0], right[1], right[0]], axis=0)
    return jnp.dot(lhs, rhs, preferred_element_type=F32)


def kernel(
    x_hbm, xm_hbm, gm_hbm, z_out,
    x_v, xm_s, gm_s, xp, dh, dl, gh, gl, gacc, x_recv, p_send, p_recv, m_send, m_recv,
    zacc, in_sem, send_sem, recv_sem, left_here,
):
    rows, cols = lax.axis_size("row"), lax.axis_size("col")
    flat = lax.axis_index("row") * cols + lax.axis_index("col")
    there = []
    for step in (rows * cols - 1, 1):
        other = lax.rem(flat + step, rows * cols)
        there.append((lax.div(other, cols), lax.rem(other, cols)))

    first_two = flat < 2
    barrier = pltpu.get_barrier_semaphore()
    pl.semaphore_signal(barrier, inc=1, device_id=there[0], device_id_type=MESH)
    replies = jnp.logical_or(flat == 0, flat == rows * cols - 1)

    @pl.when(jnp.logical_not(replies))
    def _():
        pl.semaphore_signal(barrier, inc=1, device_id=there[1], device_id_type=MESH)

    loads = [pltpu.make_async_copy(x_hbm.at[i], x_v.at[i], in_sem.at[i]) for i in range(ROWS)]
    mask_loads = [pltpu.make_async_copy(xm_hbm, xm_s, in_sem.at[ROWS]), pltpu.make_async_copy(gm_hbm, gm_s, in_sem.at[ROWS + 1])]
    for load in mask_loads:
        load.start()
    for i in (3, 4, 5, 0, 1, 2):
        loads[i].start()
    for buffer in (dh, dl):
        buffer[...] = jnp.zeros_like(buffer)

    @pl.when(replies)
    def _():
        pl.semaphore_wait(barrier, jnp.where(flat == 0, 1, 2))
        pl.semaphore_signal(left_here, inc=1, device_id=there[1], device_id_type=MESH)

    lane = lax.broadcasted_iota(jnp.int32, (1, 128), 1)
    low = lane < BS

    def window_mask(mask, i):
        def factor(t):
            return mask[i, t].astype(F32) if 0 <= t < W else jnp.float32(0)

        first = -(i % 2)
        return jnp.concatenate(
            [jnp.where(low, factor(first + 2 * u), factor(first + 2 * u + 1)) for u in range(4)], axis=1
        )

    pieces = [
        [
            (xp.at[0, :, 0:384], x_recv.at[1, 0]),
            (xp.at[1, :, 128:384], x_recv.at[1, 1, :, 128:384]),
            (xp.at[2, :, 0:256], x_recv.at[1, 2, :, 128:384]),
            (m_send.at[0], m_recv.at[1]),
            (p_send.at[0], p_recv.at[1]),
        ],
        [
            (xp.at[5, :, 128:512], x_recv.at[0, 2]),
            (xp.at[4, :, 128:384], x_recv.at[0, 1, :, 0:256]),
            (xp.at[3, :, 256:512], x_recv.at[0, 0, :, 0:256]),
            (m_send.at[1], m_recv.at[0]),
            (p_send.at[1], p_recv.at[0]),
        ],
    ]

    def remote(side, number, from_side):
        src, dst = pieces[side][number]
        return pltpu.make_async_remote_copy(
            src_ref=src, dst_ref=dst, send_sem=send_sem.at[side, number], recv_sem=recv_sem.at[from_side, number],
            device_id=there[side], device_id_type=MESH,
        )

    sends = [[remote(side, number, 1 - side) for number in range(5)] for side in (0, 1)]

    def arrived(side, number):
        remote(1 - side, number, side).wait_recv()

    blank = jnp.zeros((BS, BS), F32)

    def prepare(i):
        loads[i].wait()
        value = x_v[i]
        value = jnp.concatenate([value, blank] if i % 2 == 0 else [blank, value], axis=1) * window_mask(xm_s, i)
        xp[i] = value
        high, rest = split(value)
        span = slice(192 + 64 * i, 256 + 64 * i), slice(128 * (i // 2), 128 * (i // 2) + 512)
        dh[span] = high
        dl[span] = rest

    def pattern_row(side, r, t):
        skipped = (0, 2) if side == 0 else (2, 0)
        return None if (r, t) == skipped else 32 + 3 * r + t - (3 * r + t > 3 * skipped[0] + skipped[1])

    def put_pattern(side, i):
        ours = window_mask(gm_s, i)
        for t in range(3):
            row = pattern_row(1 - side, i % 3, t)
            start = 128 * (t + 3 * side - i // 2)
            if row is not None:
                m_send[side, row : row + 1] = ours[:, start : start + 128]

    def pack(value):
        half = value.shape[0] // 2
        return value[:half] + pltpu.roll(value[half:], 64, 1)

    def unpack(value, side):
        value = jnp.concatenate([value, pltpu.roll(value, 64, 1)], axis=0)
        return jnp.where(low, value, 0.0) if side == 0 else jnp.where(low, 0.0, value)

    def d(row, height, column, width):
        span = slice(row, row + height), slice(column, column + width)
        return dh[span], dl[span]

    def g(row, height, column, width):
        span = slice(row, row + height), slice(column, column + width)
        return gh[span], gl[span]

    for load in mask_loads:
        load.wait()
    for i in (3, 4, 5):
        prepare(i)
        put_pattern(1, i)
    m_send[1, 0:32] = pack(xp[4, :, 384:512])

    @pl.when(jnp.logical_not(replies))
    def _():
        pl.semaphore_wait(barrier, jnp.where(flat == 1, 1, 2))

    for number in range(4):
        sends[1][number].start()
    for i in (0, 1, 2):
        prepare(i)
        put_pattern(0, i)
    m_send[0, 0:32] = pack(xp[1, :, 0:128])

    @pl.when(jnp.logical_not(first_two))
    def _():
        for number in range(4):
            sends[0][number].start()

    to_right = product(d(384, 192, 128, 256), d(128, 256, 384, 256))
    p_send[1, 0:192] = to_right[:, :128]
    p_send[1, 192:288] = pack(to_right[:, 128:])
    sends[1][4].start()
    to_left = product(d(192, 192, 384, 256), d(384, 256, 128, 256))
    p_send[0, 0:192] = to_left[:, 128:]
    p_send[0, 192:288] = pack(to_left[:, :128])

    @pl.when(jnp.logical_not(first_two))
    def _():
        sends[0][4].start()

    for buffer in (gh, gl):
        buffer[...] = jnp.zeros_like(buffer)
    for p in range(3):
        gacc[p] = product(d(192 + 128 * p, 128, 256, 256), d(256, 256, 128 * p, 512))

    def put_g(row, column, value):
        high, rest = split(value)
        span = slice(row, row + value.shape[0]), slice(column, column + value.shape[1])
        gh[span] = high
        gl[span] = rest

    def put_pair(p, value):
        for i in (2 * p, 2 * p + 1):
            put_g(192 + 64 * i, 128 * p, value[64 * (i % 2) : 64 * (i % 2) + 64] * window_mask(gm_s, i))

    def take_x(side):
        for number in range(4):
            arrived(side, number)
        half = unpack(m_recv[side, 0:32], side)
        if side == 0:
            values = [
                (0, x_recv[0, 0, :, 0:256]),
                (0, jnp.concatenate([x_recv[0, 1, :, 0:256], half], axis=1)),
                (0, x_recv[0, 2]),
            ]
        else:
            values = [
                (384, x_recv[1, 0]),
                (384, jnp.concatenate([half, x_recv[1, 1, :, 128:384]], axis=1)),
                (512, x_recv[1, 2, :, 128:384]),
            ]
        for r, (column, value) in enumerate(values):
            high, rest = split(value)
            span = slice(64 * r + 576 * side, 64 * r + 576 * side + 64), slice(column, column + value.shape[1])
            dh[span] = high
            dl[span] = rest

    def take_p(side, halo):
        arrived(side, 4)
        whole = p_recv[side, 0:192]
        half = unpack(p_recv[side, 192:288], side)
        sums = [halo[:, 0:128], halo[:, 128:256] + half, halo[:, 256:384]]
        sums[2 * side] += whole
        for r in range(3):
            for t in range(3):
                row = pattern_row(side, r, t)
                if row is not None:
                    put_g(64 * r + 576 * side, 384 * side + 128 * t, sums[t][64 * r : 64 * r + 64] * m_recv[side, row : row + 1])

    def finish(p, cubic):
        for i in (2 * p, 2 * p + 1):
            start = 64 * (i % 2)
            z = 1.5 * xp[i] - (0.5 * window_mask(xm_s, i)) * cubic[start : start + 64]
            z_out[i] = z[:, start : start + W * BS]

    def over(side):
        take_x(side)
        if side == 0:
            outer = product(d(0, 448, 0, 256), d(0, 256, 0, 512))
            return outer[192:320], outer[320:448, 128:512], outer[0:192, 0:384]
        outer = product(d(320, 448, 512, 256), d(512, 256, 256, 512))
        return outer[128:256], outer[0:128, 0:384], outer[256:448, 128:512]

    def halo_over(side):
        if side == 0:
            return product(d(0, 192, 256, 256), d(256, 256, 0, 384))
        return product(d(576, 192, 256, 256), d(256, 256, 384, 384))

    def cubic_over(side):
        if side == 0:
            cubic = product(d(192, 256, 0, 256), g(0, 256, 0, 512))
            return cubic[0:128], cubic[128:256, 128:512]
        cubic = product(d(320, 256, 512, 256), g(512, 256, 256, 512))
        return cubic[128:256], cubic[0:128, 0:384]

    def cubic_within(p):
        return product(d(192 + 128 * p, 128, 256, 256), g(256, 256, 128 * p, 512))

    def both_sides(first):
        last = 1 - first
        near, far = (slice(0, 384), slice(128, 512)) if first == 0 else (slice(128, 512), slice(0, 384))
        edge, middle, halo = over(first)
        gacc[1, :, near] += middle
        put_pair(2 * first, gacc[2 * first] + edge)
        take_p(first, halo + halo_over(first))
        edge, middle = cubic_over(first)
        zacc[2 * first] = edge
        zacc[1] = jnp.zeros((128, 512), F32)
        zacc[1, :, near] = middle

        @pl.when(first_two)
        def _():
            pl.semaphore_wait(left_here, 1)
            for number in range(5):
                sends[0][number].start()

        edge, middle, halo = over(last)
        put_pair(2 * last, gacc[2 * last] + edge)
        gacc[1, :, far] += middle
        put_pair(1, gacc[1])
        halo += halo_over(last)
        finish(2 * first, zacc[2 * first] + cubic_within(2 * first))
        zacc[2 * last] = cubic_within(2 * last)
        zacc[1] += cubic_within(1)
        take_p(last, halo)
        edge, middle = cubic_over(last)
        finish(2 * last, zacc[2 * last] + edge)
        zacc[1, :, far] += middle
        finish(1, zacc[1])

    right_last = jnp.logical_and(lax.rem(flat, 2) == 1, flat != 1)

    @pl.when(jnp.logical_not(right_last))
    def _():
        both_sides(1)

    @pl.when(right_last)
    def _():
        both_sides(0)

    for side in (0, 1):
        for copy in sends[side]:
            copy.wait_send()


def body(x_band, x_mask, g_mask):
    return pl.pallas_call(
        kernel,
        out_shape=jax.ShapeDtypeStruct(x_band.shape, F32),
        in_specs=[pl.BlockSpec(memory_space=pltpu.HBM)] * 3,
        out_specs=pl.BlockSpec(memory_space=pltpu.VMEM),
        scratch_shapes=[
            pltpu.VMEM((ROWS, BS, W * BS), F32),
            pltpu.SMEM((ROWS, W), jnp.int32),
            pltpu.SMEM((ROWS, W), jnp.int32),
            pltpu.VMEM((ROWS, BS, 512), F32),
            pltpu.VMEM((768, 768), BF16),
            pltpu.VMEM((768, 768), BF16),
            pltpu.VMEM((768, 768), BF16),
            pltpu.VMEM((768, 768), BF16),
            pltpu.VMEM((3, 128, 512), F32),
            pltpu.VMEM((2, 3, BS, 384), F32),
            pltpu.VMEM((2, 288, 128), F32),
            pltpu.VMEM((2, 288, 128), F32),
            pltpu.VMEM((2, 40, 128), F32),
            pltpu.VMEM((2, 40, 128), F32),
            pltpu.VMEM((3, 128, 512), F32),
            pltpu.SemaphoreType.DMA((ROWS + 2,)),
            pltpu.SemaphoreType.DMA((2, 5)),
            pltpu.SemaphoreType.DMA((2, 5)),
            pltpu.SemaphoreType.REGULAR,
        ],
        compiler_params=pltpu.CompilerParams(
            collective_id=0, has_side_effects=True, vmem_limit_bytes=48 * 1024 * 1024
        ),
        cost_estimate=pl.CostEstimate(flops=1_000_000_000, bytes_accessed=1_500_000, transcendentals=0),
    )(*(pltpu.with_memory_space_constraint(a, pltpu.HBM) for a in (x_band, x_mask, g_mask)))


def solution(mesh):
    placed = (P(("row", "col"), None, None), P(("row", "col"), None), P(("row", "col"), None))
    return jax.shard_map(
        body, mesh=mesh, in_specs=placed, out_specs=P(("row", "col"), None, None), check_vma=False
    )
```

```python
import functools

import jax
import jax.numpy as jnp
from jax import lax
from jax.experimental import pallas as pl
from jax.experimental.pallas import tpu as pltpu
from jax.sharding import PartitionSpec as P

BS = 64
W = 7
ROWS = 6
MESH = pl.DeviceIdType.MESH
F32 = jnp.float32
BF16 = jnp.bfloat16


def split(value):
    high = value.astype(BF16)
    return high, (value - high.astype(F32)).astype(BF16)


def product(left, right):
    lhs = jnp.concatenate([left[0], left[0], left[1]], axis=1)
    rhs = jnp.concatenate([right[0], right[1], right[0]], axis=0)
    return jnp.dot(lhs, rhs, preferred_element_type=F32)


def works_right_last(flat):
    return jnp.logical_and(lax.rem(flat, 2) == 1, flat != 1)


def kernel(
    x_hbm, xm_hbm, gm_hbm, done, part, scale, eh, el, hh, hl,
    x_v, xm_s, gm_s, xp, dh, dl, gh, gl, gacc, x_recv, p_send, p_recv, m_send, m_recv,
    zacc, in_sem, send_sem, recv_sem, left_here,
):
    rows, cols = lax.axis_size("row"), lax.axis_size("col")
    flat = lax.axis_index("row") * cols + lax.axis_index("col")
    there = []
    for step in (rows * cols - 1, 1):
        other = lax.rem(flat + step, rows * cols)
        there.append((lax.div(other, cols), lax.rem(other, cols)))

    first_two = flat < 2
    barrier = pltpu.get_barrier_semaphore()
    pl.semaphore_signal(barrier, inc=1, device_id=there[0], device_id_type=MESH)
    replies = jnp.logical_or(flat == 0, flat == rows * cols - 1)

    @pl.when(jnp.logical_not(replies))
    def _():
        pl.semaphore_signal(barrier, inc=1, device_id=there[1], device_id_type=MESH)

    loads = [pltpu.make_async_copy(x_hbm.at[i], x_v.at[i], in_sem.at[i]) for i in range(ROWS)]
    mask_loads = [pltpu.make_async_copy(xm_hbm, xm_s, in_sem.at[ROWS]), pltpu.make_async_copy(gm_hbm, gm_s, in_sem.at[ROWS + 1])]
    for load in mask_loads:
        load.start()
    for i in (5, 4, 3, 0, 1, 2):
        loads[i].start()
    for buffer in (dh, dl):
        buffer[...] = jnp.zeros_like(buffer)

    @pl.when(replies)
    def _():
        pl.semaphore_wait(barrier, jnp.where(flat == 0, 1, 2))
        pl.semaphore_signal(left_here, inc=1, device_id=there[1], device_id_type=MESH)

    lane = lax.broadcasted_iota(jnp.int32, (1, 128), 1)
    low = lane < BS

    def window_mask(mask, i):
        def factor(t):
            return mask[i, t].astype(F32) if 0 <= t < W else jnp.float32(0)

        first = -(i % 2)
        return jnp.concatenate(
            [jnp.where(low, factor(first + 2 * u), factor(first + 2 * u + 1)) for u in range(4)], axis=1
        )

    pieces = [
        [
            (xp.at[0, :, 0:384], x_recv.at[1, 0]),
            (xp.at[1, :, 128:384], x_recv.at[1, 1, :, 128:384]),
            (xp.at[2, :, 0:256], x_recv.at[1, 2, :, 128:384]),
            (m_send.at[0], m_recv.at[1]),
            (p_send.at[0], p_recv.at[1]),
        ],
        [
            (xp.at[5, :, 128:512], x_recv.at[0, 2]),
            (xp.at[4, :, 128:384], x_recv.at[0, 1, :, 0:256]),
            (xp.at[3, :, 256:512], x_recv.at[0, 0, :, 0:256]),
            (m_send.at[1], m_recv.at[0]),
            (p_send.at[1], p_recv.at[0]),
        ],
    ]

    def remote(side, number, from_side):
        src, dst = pieces[side][number]
        return pltpu.make_async_remote_copy(
            src_ref=src, dst_ref=dst, send_sem=send_sem.at[side, number], recv_sem=recv_sem.at[from_side, number],
            device_id=there[side], device_id_type=MESH,
        )

    sends = [[remote(side, number, 1 - side) for number in range(5)] for side in (0, 1)]

    def arrived(side, number):
        remote(1 - side, number, side).wait_recv()

    blank = jnp.zeros((BS, BS), F32)

    def prepare(i):
        loads[i].wait()
        value = x_v[i]
        value = jnp.concatenate([value, blank] if i % 2 == 0 else [blank, value], axis=1) * window_mask(xm_s, i)
        xp[i] = value
        high, rest = split(value)
        span = slice(192 + 64 * i, 256 + 64 * i), slice(128 * (i // 2), 128 * (i // 2) + 512)
        dh[span] = high
        dl[span] = rest

    def pattern_row(side, r, t):
        skipped = (0, 2) if side == 0 else (2, 0)
        return None if (r, t) == skipped else 32 + 3 * r + t - (3 * r + t > 3 * skipped[0] + skipped[1])

    def put_pattern(side, i):
        ours = window_mask(gm_s, i)
        for t in range(3):
            row = pattern_row(1 - side, i % 3, t)
            start = 128 * (t + 3 * side - i // 2)
            if row is not None:
                m_send[side, row : row + 1] = ours[:, start : start + 128]

    def pack(value):
        half = value.shape[0] // 2
        return value[:half] + pltpu.roll(value[half:], 64, 1)

    def unpack(value, side):
        value = jnp.concatenate([value, pltpu.roll(value, 64, 1)], axis=0)
        return jnp.where(low, value, 0.0) if side == 0 else jnp.where(low, 0.0, value)

    def d(row, height, column, width):
        span = slice(row, row + height), slice(column, column + width)
        return dh[span], dl[span]

    def g(row, height, column, width):
        span = slice(row, row + height), slice(column, column + width)
        return gh[span], gl[span]

    for load in mask_loads:
        load.wait()

    @pl.when(jnp.logical_not(replies))
    def _():
        pl.semaphore_wait(barrier, jnp.where(flat == 1, 1, 2))

    for number, i in enumerate((5, 4, 3)):
        prepare(i)
        sends[1][number].start()
        put_pattern(1, i)
    m_send[1, 0:32] = pack(xp[4, :, 384:512])
    sends[1][3].start()
    for i in (0, 1, 2):
        prepare(i)
        put_pattern(0, i)
    m_send[0, 0:32] = pack(xp[1, :, 0:128])

    @pl.when(jnp.logical_not(first_two))
    def _():
        for number in range(4):
            sends[0][number].start()

    to_right = product(d(384, 192, 128, 256), d(128, 256, 384, 256))
    p_send[1, 0:192] = to_right[:, :128]
    p_send[1, 192:288] = pack(to_right[:, 128:])
    sends[1][4].start()
    to_left = product(d(192, 192, 384, 256), d(384, 256, 128, 256))
    p_send[0, 0:192] = to_left[:, 128:]
    p_send[0, 192:288] = pack(to_left[:, :128])

    @pl.when(jnp.logical_not(first_two))
    def _():
        sends[0][4].start()

    for buffer in (gh, gl):
        buffer[...] = jnp.zeros_like(buffer)
    for p in range(3):
        gacc[p] = product(d(192 + 128 * p, 128, 256, 256), d(256, 256, 128 * p, 512))

    def put_g(row, column, value):
        high, rest = split(value)
        span = slice(row, row + value.shape[0]), slice(column, column + value.shape[1])
        gh[span] = high
        gl[span] = rest

    def put_pair(p, value):
        for i in (2 * p, 2 * p + 1):
            put_g(192 + 64 * i, 128 * p, value[64 * (i % 2) : 64 * (i % 2) + 64] * window_mask(gm_s, i))

    def take_x(side):
        for number in range(4):
            arrived(side, number)
        half = unpack(m_recv[side, 0:32], side)
        if side == 0:
            values = [
                (0, x_recv[0, 0, :, 0:256]),
                (0, jnp.concatenate([x_recv[0, 1, :, 0:256], half], axis=1)),
                (0, x_recv[0, 2]),
            ]
        else:
            values = [
                (384, x_recv[1, 0]),
                (384, jnp.concatenate([half, x_recv[1, 1, :, 128:384]], axis=1)),
                (512, x_recv[1, 2, :, 128:384]),
            ]
        for r, (column, value) in enumerate(values):
            high, rest = split(value)
            span = slice(64 * r + 576 * side, 64 * r + 576 * side + 64), slice(column, column + value.shape[1])
            dh[span] = high
            dl[span] = rest

    def take_p(side, halo, put, place):
        arrived(side, 4)
        whole = p_recv[side, 0:192]
        half = unpack(p_recv[side, 192:288], side)
        sums = [halo[:, 0:128], halo[:, 128:256] + half, halo[:, 256:384]]
        sums[2 * side] += whole
        for r in range(3):
            for t in range(3):
                row = pattern_row(side, r, t)
                if row is not None:
                    put(64 * r + place[0], 128 * t + place[1], sums[t][64 * r : 64 * r + 64] * m_recv[side, row : row + 1])

    def put_h(row, column, value):
        high, rest = split(value)
        span = slice(row, row + 64), slice(column, column + 128)
        hh[span] = high
        hl[span] = rest

    def finish(p, cubic, last):
        for i in (2 * p, 2 * p + 1):
            start = 64 * (i % 2)
            half = 0.5 * window_mask(xm_s, i)
            z = 1.5 * xp[i] - half * cubic[start : start + 64]
            if i // 3 == last:
                part[i % 3] = z
                scale[i % 3 : i % 3 + 1] = half
            else:
                done[i % 3] = z[:, start : start + W * BS]

    def over(side):
        take_x(side)
        if side == 0:
            outer = product(d(0, 448, 0, 256), d(0, 256, 0, 512))
            return outer[192:320], outer[320:448, 128:512], outer[0:192, 0:384]
        outer = product(d(320, 448, 512, 256), d(512, 256, 256, 512))
        return outer[128:256], outer[0:128, 0:384], outer[256:448, 128:512]

    def halo_over(side):
        if side == 0:
            return product(d(0, 192, 256, 256), d(256, 256, 0, 384))
        return product(d(576, 192, 256, 256), d(256, 256, 384, 384))

    def cubic_over(side):
        if side == 0:
            cubic = product(d(192, 256, 0, 256), g(0, 256, 0, 512))
            return cubic[0:128], cubic[128:256, 128:512]
        cubic = product(d(320, 256, 512, 256), g(512, 256, 256, 512))
        return cubic[128:256], cubic[0:128, 0:384]

    def cubic_within(p):
        return product(d(192 + 128 * p, 128, 256, 256), g(256, 256, 128 * p, 512))

    def both_sides(first):
        last = 1 - first
        near, far = (slice(0, 384), slice(128, 512)) if first == 0 else (slice(128, 512), slice(0, 384))
        edge, middle, halo = over(first)
        gacc[1, :, near] += middle
        put_pair(2 * first, gacc[2 * first] + edge)
        take_p(first, halo + halo_over(first), put_g, (576 * first, 384 * first))
        edge, middle = cubic_over(first)
        zacc[2 * first] = edge
        zacc[1] = jnp.zeros((128, 512), F32)
        zacc[1, :, near] = middle

        @pl.when(first_two)
        def _():
            pl.semaphore_wait(left_here, 1)
            for number in range(5):
                sends[0][number].start()

        edge, middle, halo = over(last)
        put_pair(2 * last, gacc[2 * last] + edge)
        gacc[1, :, far] += middle
        put_pair(1, gacc[1])
        finish(2 * first, zacc[2 * first] + cubic_within(2 * first), last)
        edge, middle = cubic_over(last)
        finish(2 * last, edge + cubic_within(2 * last), last)
        zacc[1] += cubic_within(1)
        zacc[1, :, far] += middle
        finish(1, zacc[1], last)
        halo += halo_over(last)
        e = d(192 + 192 * last, 192, 512 * last, 256)
        eh[...] = e[0]
        el[...] = e[1]
        for half in (hh, hl):
            half[...] = jnp.zeros_like(half)
        take_p(last, halo, put_h, (64 * last, 0))

    right_last = works_right_last(flat)

    @pl.when(jnp.logical_not(right_last))
    def _():
        both_sides(1)

    @pl.when(right_last)
    def _():
        both_sides(0)

    for side in (0, 1):
        for copy in sends[side]:
            copy.wait_send()


def closing(done, part, scale, eh, el, hh, hl, z_hbm, z_v, sem):
    right_last = works_right_last(lax.axis_index("row") * lax.axis_size("col") + lax.axis_index("col"))

    def write(last):
        stores = [pltpu.make_async_copy(done, z_hbm.at[3 - 3 * last : 6 - 3 * last], sem.at[3])]
        stores[0].start()
        cubic = product((eh[...], el[...]), (hh[...], hl[...]))
        for r in range(3):
            i = 3 * last + r
            shift = 128 * (3 * last - i // 2)
            term = cubic[64 * r : 64 * r + 64]
            if shift < 0:
                term = jnp.concatenate([term[:, -shift:], jnp.zeros((BS, 128 - shift), F32)], axis=1)
            elif shift == 0:
                term = jnp.concatenate([term, jnp.zeros((BS, 128), F32)], axis=1)
            else:
                term = jnp.concatenate([jnp.zeros((BS, shift), F32), term[:, : 512 - shift]], axis=1)
            z = part[r] - scale[r : r + 1] * term
            z_v[r] = z[:, 64 * (i % 2) : 64 * (i % 2) + W * BS]
            stores.append(pltpu.make_async_copy(z_v.at[r], z_hbm.at[i], sem.at[r]))
            stores[-1].start()
        for store in stores:
            store.wait()

    @pl.when(jnp.logical_not(right_last))
    def _():
        write(0)

    @pl.when(right_last)
    def _():
        write(1)


def body(x_band, x_mask, g_mask):
    shapes = [
        ((3, BS, W * BS), F32), ((3, BS, 512), F32), ((8, 512), F32),
        ((192, 256), BF16), ((192, 256), BF16), ((256, 384), BF16), ((256, 384), BF16),
    ]
    between = pl.pallas_call(
        kernel,
        out_shape=[jax.ShapeDtypeStruct(*shape) for shape in shapes],
        in_specs=[pl.BlockSpec(memory_space=pltpu.HBM)] * 3,
        out_specs=[pl.BlockSpec(memory_space=pltpu.VMEM)] * len(shapes),
        scratch_shapes=[
            pltpu.VMEM((ROWS, BS, W * BS), F32),
            pltpu.SMEM((ROWS, W), jnp.int32),
            pltpu.SMEM((ROWS, W), jnp.int32),
            pltpu.VMEM((ROWS, BS, 512), F32),
            pltpu.VMEM((768, 768), BF16),
            pltpu.VMEM((768, 768), BF16),
            pltpu.VMEM((768, 768), BF16),
            pltpu.VMEM((768, 768), BF16),
            pltpu.VMEM((3, 128, 512), F32),
            pltpu.VMEM((2, 3, BS, 384), F32),
            pltpu.VMEM((2, 288, 128), F32),
            pltpu.VMEM((2, 288, 128), F32),
            pltpu.VMEM((2, 40, 128), F32),
            pltpu.VMEM((2, 40, 128), F32),
            pltpu.VMEM((3, 128, 512), F32),
            pltpu.SemaphoreType.DMA((ROWS + 2,)),
            pltpu.SemaphoreType.DMA((2, 5)),
            pltpu.SemaphoreType.DMA((2, 5)),
            pltpu.SemaphoreType.REGULAR,
        ],
        compiler_params=pltpu.CompilerParams(
            collective_id=0, has_side_effects=True, vmem_limit_bytes=48 * 1024 * 1024
        ),
        cost_estimate=pl.CostEstimate(flops=1_000_000_000, bytes_accessed=1_500_000, transcendentals=0),
    )(*(pltpu.with_memory_space_constraint(a, pltpu.HBM) for a in (x_band, x_mask, g_mask)))
    return pl.pallas_call(
        closing,
        out_shape=jax.ShapeDtypeStruct(x_band.shape, F32),
        in_specs=[pl.BlockSpec(memory_space=pltpu.VMEM)] * len(shapes),
        out_specs=pl.BlockSpec(memory_space=pltpu.HBM),
        scratch_shapes=[pltpu.VMEM((3, BS, W * BS), F32), pltpu.SemaphoreType.DMA((4,))],
        compiler_params=pltpu.CompilerParams(vmem_limit_bytes=16 * 1024 * 1024),
    )(*(pltpu.with_memory_space_constraint(a, pltpu.VMEM) for a in between))


def solution(mesh):
    placed = (P(("row", "col"), None, None), P(("row", "col"), None), P(("row", "col"), None))
    return jax.shard_map(
        body, mesh=mesh, in_specs=placed, out_specs=P(("row", "col"), None, None), check_vma=False
    )
```

```python
import functools

import jax
import jax.numpy as jnp
from jax import lax
from jax.experimental import pallas as pl
from jax.experimental.pallas import tpu as pltpu
from jax.sharding import PartitionSpec as P

BS = 64
W = 7
ROWS = 6
MESH = pl.DeviceIdType.MESH
F32 = jnp.float32
BF16 = jnp.bfloat16


def split(value):
    high = value.astype(BF16)
    return high, (value - high.astype(F32)).astype(BF16)


def product(left, right):
    lhs = jnp.concatenate([left[0], left[0], left[1]], axis=1)
    rhs = jnp.concatenate([right[0], right[1], right[0]], axis=0)
    return jnp.dot(lhs, rhs, preferred_element_type=F32)


def works_right_last(flat):
    return jnp.logical_and(lax.rem(flat, 2) == 1, flat != 1)


def kernel(
    x_hbm, xm_hbm, gm_hbm, done, part, scale, eh, el, hh, hl,
    x_v, xm_s, gm_s, xp, dh, dl, gh, gl, gacc, x_recv, p_send, p_recv, m_send, m_recv,
    zacc, in_sem, send_sem, recv_sem, left_here,
):
    rows, cols = lax.axis_size("row"), lax.axis_size("col")
    flat = lax.axis_index("row") * cols + lax.axis_index("col")
    there = []
    for step in (rows * cols - 1, 1):
        other = lax.rem(flat + step, rows * cols)
        there.append((lax.div(other, cols), lax.rem(other, cols)))

    first_two = flat < 2
    barrier = pltpu.get_barrier_semaphore()
    pl.semaphore_signal(barrier, inc=1, device_id=there[0], device_id_type=MESH)
    replies = jnp.logical_or(flat == 0, flat == rows * cols - 1)

    @pl.when(jnp.logical_not(replies))
    def _():
        pl.semaphore_signal(barrier, inc=1, device_id=there[1], device_id_type=MESH)

    loads = [pltpu.make_async_copy(x_hbm.at[i], x_v.at[i], in_sem.at[i]) for i in range(ROWS)]
    mask_loads = [pltpu.make_async_copy(xm_hbm, xm_s, in_sem.at[ROWS]), pltpu.make_async_copy(gm_hbm, gm_s, in_sem.at[ROWS + 1])]
    for load in mask_loads:
        load.start()
    for i in (5, 4, 3, 0, 1, 2):
        loads[i].start()
    for buffer in (dh, dl):
        buffer[...] = jnp.zeros_like(buffer)

    @pl.when(replies)
    def _():
        pl.semaphore_wait(barrier, jnp.where(flat == 0, 1, 2))
        pl.semaphore_signal(left_here, inc=1, device_id=there[1], device_id_type=MESH)

    lane = lax.broadcasted_iota(jnp.int32, (1, 128), 1)
    low = lane < BS

    def window_mask(mask, i):
        def factor(t):
            return mask[i, t].astype(F32) if 0 <= t < W else jnp.float32(0)

        first = -(i % 2)
        return jnp.concatenate(
            [jnp.where(low, factor(first + 2 * u), factor(first + 2 * u + 1)) for u in range(4)], axis=1
        )

    pieces = [
        [
            (xp.at[0, :, 0:384], x_recv.at[1, 0]),
            (xp.at[1, :, 128:384], x_recv.at[1, 1, :, 128:384]),
            (xp.at[2, :, 0:256], x_recv.at[1, 2, :, 128:384]),
            (m_send.at[0], m_recv.at[1]),
            (p_send.at[0], p_recv.at[1]),
        ],
        [
            (xp.at[5, :, 128:512], x_recv.at[0, 2]),
            (xp.at[4, :, 128:384], x_recv.at[0, 1, :, 0:256]),
            (xp.at[3, :, 256:512], x_recv.at[0, 0, :, 0:256]),
            (m_send.at[1], m_recv.at[0]),
            (p_send.at[1], p_recv.at[0]),
        ],
    ]

    def remote(side, number, from_side):
        src, dst = pieces[side][number]
        return pltpu.make_async_remote_copy(
            src_ref=src, dst_ref=dst, send_sem=send_sem.at[side, number], recv_sem=recv_sem.at[from_side, number],
            device_id=there[side], device_id_type=MESH,
        )

    sends = [[remote(side, number, 1 - side) for number in range(5)] for side in (0, 1)]

    def arrived(side, number):
        remote(1 - side, number, side).wait_recv()

    blank = jnp.zeros((BS, BS), F32)

    def prepare(i):
        loads[i].wait()
        value = x_v[i]
        value = jnp.concatenate([value, blank] if i % 2 == 0 else [blank, value], axis=1) * window_mask(xm_s, i)
        xp[i] = value
        high, rest = split(value)
        span = slice(192 + 64 * i, 256 + 64 * i), slice(128 * (i // 2), 128 * (i // 2) + 512)
        dh[span] = high
        dl[span] = rest

    def pattern_row(side, r, t):
        skipped = (0, 2) if side == 0 else (2, 0)
        return None if (r, t) == skipped else 32 + 3 * r + t - (3 * r + t > 3 * skipped[0] + skipped[1])

    def put_pattern(side, i):
        ours = window_mask(gm_s, i)
        for t in range(3):
            row = pattern_row(1 - side, i % 3, t)
            start = 128 * (t + 3 * side - i // 2)
            if row is not None:
                m_send[side, row : row + 1] = ours[:, start : start + 128]

    def pack(value):
        half = value.shape[0] // 2
        return value[:half] + pltpu.roll(value[half:], 64, 1)

    def unpack(value, side):
        value = jnp.concatenate([value, pltpu.roll(value, 64, 1)], axis=0)
        return jnp.where(low, value, 0.0) if side == 0 else jnp.where(low, 0.0, value)

    def d(row, height, column, width):
        span = slice(row, row + height), slice(column, column + width)
        return dh[span], dl[span]

    def g(row, height, column, width):
        span = slice(row, row + height), slice(column, column + width)
        return gh[span], gl[span]

    for load in mask_loads:
        load.wait()

    @pl.when(jnp.logical_not(replies))
    def _():
        pl.semaphore_wait(barrier, jnp.where(flat == 1, 1, 2))

    for number, i in enumerate((5, 4, 3)):
        prepare(i)
        sends[1][number].start()
        put_pattern(1, i)
    m_send[1, 0:32] = pack(xp[4, :, 384:512])
    sends[1][3].start()
    for i in (0, 1, 2):
        prepare(i)
        put_pattern(0, i)
    m_send[0, 0:32] = pack(xp[1, :, 0:128])

    @pl.when(jnp.logical_not(first_two))
    def _():
        for number in range(4):
            sends[0][number].start()

    to_right = product(d(384, 192, 128, 256), d(128, 256, 384, 256))
    p_send[1, 0:192] = to_right[:, :128]
    p_send[1, 192:288] = pack(to_right[:, 128:])
    sends[1][4].start()
    to_left = product(d(192, 192, 384, 256), d(384, 256, 128, 256))
    p_send[0, 0:192] = to_left[:, 128:]
    p_send[0, 192:288] = pack(to_left[:, :128])

    @pl.when(jnp.logical_not(first_two))
    def _():
        sends[0][4].start()

    for buffer in (gh, gl, hh, hl):
        buffer[...] = jnp.zeros_like(buffer)
    for p in range(3):
        gacc[p] = product(d(192 + 128 * p, 128, 256, 256), d(256, 256, 128 * p, 512))

    def put_g(row, column, value):
        high, rest = split(value)
        span = slice(row, row + value.shape[0]), slice(column, column + value.shape[1])
        gh[span] = high
        gl[span] = rest

    def put_pair(p, value):
        for i in (2 * p, 2 * p + 1):
            put_g(192 + 64 * i, 128 * p, value[64 * (i % 2) : 64 * (i % 2) + 64] * window_mask(gm_s, i))

    def take_x(side):
        for number in range(4):
            arrived(side, number)
        half = unpack(m_recv[side, 0:32], side)
        if side == 0:
            values = [
                (0, x_recv[0, 0, :, 0:256]),
                (0, jnp.concatenate([x_recv[0, 1, :, 0:256], half], axis=1)),
                (0, x_recv[0, 2]),
            ]
        else:
            values = [
                (384, x_recv[1, 0]),
                (384, jnp.concatenate([half, x_recv[1, 1, :, 128:384]], axis=1)),
                (512, x_recv[1, 2, :, 128:384]),
            ]
        for r, (column, value) in enumerate(values):
            high, rest = split(value)
            span = slice(64 * r + 576 * side, 64 * r + 576 * side + 64), slice(column, column + value.shape[1])
            dh[span] = high
            dl[span] = rest

    def take_p(side, halo, put, place):
        arrived(side, 4)
        whole = p_recv[side, 0:192]
        half = unpack(p_recv[side, 192:288], side)
        sums = [halo[:, 0:128], halo[:, 128:256] + half, halo[:, 256:384]]
        sums[2 * side] += whole
        for r in range(3):
            for t in range(3):
                row = pattern_row(side, r, t)
                if row is not None:
                    put(64 * r + place[0], 128 * t + place[1], sums[t][64 * r : 64 * r + 64] * m_recv[side, row : row + 1])

    def put_h(row, column, value):
        high, rest = split(value)
        span = slice(row, row + 64), slice(column, column + 128)
        hh[span] = high
        hl[span] = rest

    def finish(p, cubic, last):
        for i in (2 * p, 2 * p + 1):
            start = 64 * (i % 2)
            half = 0.5 * window_mask(xm_s, i)
            z = 1.5 * xp[i] - half * cubic[start : start + 64]
            if i // 3 == last:
                part[i % 3] = z
                scale[i % 3 : i % 3 + 1] = half
            else:
                done[i % 3] = z[:, start : start + W * BS]

    def over(side):
        take_x(side)
        if side == 0:
            outer = product(d(0, 448, 0, 256), d(0, 256, 0, 512))
            return outer[192:320], outer[320:448, 128:512], outer[0:192, 0:384]
        outer = product(d(320, 448, 512, 256), d(512, 256, 256, 512))
        return outer[128:256], outer[0:128, 0:384], outer[256:448, 128:512]

    def halo_over(side):
        none = jnp.zeros((64, 384), F32)
        if side == 0:
            return jnp.concatenate([none, product(d(64, 128, 256, 128), d(256, 128, 0, 384))], axis=0)
        return jnp.concatenate([product(d(576, 128, 384, 128), d(384, 128, 384, 384)), none], axis=0)

    def cubic_over(side):
        if side == 0:
            cubic = product(d(192, 256, 0, 256), g(0, 256, 0, 512))
            return cubic[0:128], cubic[128:256, 128:512]
        cubic = product(d(320, 256, 512, 256), g(512, 256, 256, 512))
        return cubic[128:256], cubic[0:128, 0:384]

    def cubic_within(p):
        return product(d(192 + 128 * p, 128, 256, 256), g(256, 256, 128 * p, 512))

    def both_sides(first):
        last = 1 - first
        near, far = (slice(0, 384), slice(128, 512)) if first == 0 else (slice(128, 512), slice(0, 384))
        edge, middle, halo = over(first)
        gacc[1, :, near] += middle
        put_pair(2 * first, gacc[2 * first] + edge)
        take_p(first, halo + halo_over(first), put_g, (576 * first, 384 * first))
        edge, middle = cubic_over(first)
        zacc[2 * first] = edge
        zacc[1] = jnp.zeros((128, 512), F32)
        zacc[1, :, near] = middle

        @pl.when(first_two)
        def _():
            pl.semaphore_wait(left_here, 1)
            for number in range(5):
                sends[0][number].start()

        edge, middle, halo = over(last)
        put_pair(2 * last, gacc[2 * last] + edge)
        gacc[1, :, far] += middle
        put_pair(1, gacc[1])
        finish(2 * first, zacc[2 * first] + cubic_within(2 * first), last)
        edge, middle = cubic_over(last)
        finish(2 * last, edge + cubic_within(2 * last), last)
        zacc[1] += cubic_within(1)
        zacc[1, :, far] += middle
        finish(1, zacc[1], last)
        halo += halo_over(last)
        e = d(192 + 192 * last, 192, 512 * last, 256)
        eh[...] = e[0]
        el[...] = e[1]
        take_p(last, halo, put_h, (64 * last, 0))

    right_last = works_right_last(flat)

    @pl.when(jnp.logical_not(right_last))
    def _():
        both_sides(1)

    @pl.when(right_last)
    def _():
        both_sides(0)

    for side in (0, 1):
        for copy in sends[side]:
            copy.wait_send()


def closing(done, part, scale, eh, el, hh, hl, z_hbm, z_v, sem):
    right_last = works_right_last(lax.axis_index("row") * lax.axis_size("col") + lax.axis_index("col"))

    def write(last):
        stores = [pltpu.make_async_copy(done, z_hbm.at[3 - 3 * last : 6 - 3 * last], sem.at[3])]
        stores[0].start()
        cubic = product((eh[...], el[...]), (hh[...], hl[...]))
        for r in range(3):
            i = 3 * last + r
            shift = 128 * (3 * last - i // 2)
            term = cubic[64 * r : 64 * r + 64]
            if shift < 0:
                term = jnp.concatenate([term[:, -shift:], jnp.zeros((BS, 128 - shift), F32)], axis=1)
            elif shift == 0:
                term = jnp.concatenate([term, jnp.zeros((BS, 128), F32)], axis=1)
            else:
                term = jnp.concatenate([jnp.zeros((BS, shift), F32), term[:, : 512 - shift]], axis=1)
            z = part[r] - scale[r : r + 1] * term
            z_v[r] = z[:, 64 * (i % 2) : 64 * (i % 2) + W * BS]
            stores.append(pltpu.make_async_copy(z_v.at[r], z_hbm.at[i], sem.at[r]))
            stores[-1].start()
        for store in stores:
            store.wait()

    @pl.when(jnp.logical_not(right_last))
    def _():
        write(0)

    @pl.when(right_last)
    def _():
        write(1)


def body(x_band, x_mask, g_mask):
    shapes = [
        ((3, BS, W * BS), F32), ((3, BS, 512), F32), ((8, 512), F32),
        ((192, 256), BF16), ((192, 256), BF16), ((256, 384), BF16), ((256, 384), BF16),
    ]
    between = pl.pallas_call(
        kernel,
        out_shape=[jax.ShapeDtypeStruct(*shape) for shape in shapes],
        in_specs=[pl.BlockSpec(memory_space=pltpu.HBM)] * 3,
        out_specs=[pl.BlockSpec(memory_space=pltpu.VMEM)] * len(shapes),
        scratch_shapes=[
            pltpu.VMEM((ROWS, BS, W * BS), F32),
            pltpu.SMEM((ROWS, W), jnp.int32),
            pltpu.SMEM((ROWS, W), jnp.int32),
            pltpu.VMEM((ROWS, BS, 512), F32),
            pltpu.VMEM((768, 768), BF16),
            pltpu.VMEM((768, 768), BF16),
            pltpu.VMEM((768, 768), BF16),
            pltpu.VMEM((768, 768), BF16),
            pltpu.VMEM((3, 128, 512), F32),
            pltpu.VMEM((2, 3, BS, 384), F32),
            pltpu.VMEM((2, 288, 128), F32),
            pltpu.VMEM((2, 288, 128), F32),
            pltpu.VMEM((2, 40, 128), F32),
            pltpu.VMEM((2, 40, 128), F32),
            pltpu.VMEM((3, 128, 512), F32),
            pltpu.SemaphoreType.DMA((ROWS + 2,)),
            pltpu.SemaphoreType.DMA((2, 5)),
            pltpu.SemaphoreType.DMA((2, 5)),
            pltpu.SemaphoreType.REGULAR,
        ],
        compiler_params=pltpu.CompilerParams(
            collective_id=0, has_side_effects=True, vmem_limit_bytes=48 * 1024 * 1024
        ),
        cost_estimate=pl.CostEstimate(flops=1_000_000_000, bytes_accessed=1_500_000, transcendentals=0),
    )(*(pltpu.with_memory_space_constraint(a, pltpu.HBM) for a in (x_band, x_mask, g_mask)))
    return pl.pallas_call(
        closing,
        out_shape=jax.ShapeDtypeStruct(x_band.shape, F32),
        in_specs=[pl.BlockSpec(memory_space=pltpu.VMEM)] * len(shapes),
        out_specs=pl.BlockSpec(memory_space=pltpu.HBM),
        scratch_shapes=[pltpu.VMEM((3, BS, W * BS), F32), pltpu.SemaphoreType.DMA((4,))],
        compiler_params=pltpu.CompilerParams(vmem_limit_bytes=16 * 1024 * 1024),
    )(*(pltpu.with_memory_space_constraint(a, pltpu.VMEM) for a in between))


def solution(mesh):
    placed = (P(("row", "col"), None, None), P(("row", "col"), None), P(("row", "col"), None))
    return jax.shard_map(
        body, mesh=mesh, in_specs=placed, out_specs=P(("row", "col"), None, None), check_vma=False
    )
```
